32 devices in a mesh: seq: 4 (over x, core), blk: 8 (over z, y).
Axes of the slice: x: 2, y: 2, z: 4, core: 2. Of those that a mesh axis runs over, the one named last changes fastest.
Arguments:
- tokens: bfloat16 [4096, 8192], P('seq', 'blk'), may hold values from -6 to 6
- up_in: bfloat16 [32, 256, 1024], P('blk'), may hold values from -0.375 to 0.375
- up_out: bfloat16 [32, 1024, 1024], P('blk'), may hold values from -0.1875 to 0.1875
- down_in: bfloat16 [32, 1024, 1024], P('blk'), may hold values from -0.1875 to 0.1875
- down_out: bfloat16 [32, 256, 1024], P('blk'), may hold values from -0.1875 to 0.1875
- cotangent: bfloat16 [4096, 8192], P('seq', 'blk'), may hold values from -6 to 6
Outputs:
- mlp_out: bfloat16 [4096, 8192], P('seq', 'blk')
- input_grad: bfloat16 [4096, 8192], P('seq', 'blk')
- weight_grads: float32 [32, 2560, 1024], P('blk', 'seq')
The draws below stay inside these ranges and needn't reach their ends.
All inputs are finite; a program needn't handle non-finite values.
Results may differ from the reference program's by a relative error of at most 0.009.
Values may be sent and summed in bfloat16 or wider, within the bound.
No kernel may reach another device: no remote copies, remote signals or barrier semaphores. Data moves between devices by JAX's collectives and lax.ppermute only.
A program may use at most 192 MiB of HBM per device.

```python
import jax
import jax.numpy as jnp
from jax import lax

B = 256
NB = 32
TOK_DEV = 1024
D = 8192
E = 1024
TOKENS = 4096
N_SEQ = 4


def shard_levels(own_key, shape, cuts, least, largest):
    factor_of, own = 1.0, jax.random.fold_in(own_key, 6)
    for axis_at, parts in cuts:
        draws = jnp.exp(jax.random.uniform(jax.random.fold_in(own, axis_at), (parts,), jnp.float32, least / len(cuts), largest / len(cuts)))
        factor_of = factor_of * jnp.repeat(draws, shape[axis_at] // parts).reshape([-1 if axis == axis_at else 1 for axis in range(len(shape))])
    return factor_of


def noise(key, shape, deviation, most, pieces=(), held_as=jnp.bfloat16):
    values = deviation * jax.random.normal(key, shape, jnp.float32)
    if pieces:
        values = values * shard_levels(key, shape, pieces, -0.22, 0.18)
    return jnp.clip(values, -most, most).astype(held_as)


def setup_inputs(seed: int = 0) -> dict:
    key_of = jax.random.split(jax.random.key(seed), 7)
    return {
        "tokens": noise(key_of[0], (TOKENS, D), 1.0, 6.0, ((0, 4), (1, 8))),
        "up_in": noise(key_of[1], (NB, B, E), B ** -0.5, 0.375, ((0, 8),)),
        "up_out": noise(key_of[2], (NB, E, E), E ** -0.5, 0.1875, ((0, 8),)),
        "down_in": noise(key_of[3], (NB, E, E), E ** -0.5, 0.1875, ((0, 8),)),
        "down_out": noise(key_of[4], (NB, B, E), E ** -0.5, 0.1875, ((0, 8),)),
        "cotangent": noise(key_of[5], (TOKENS, D), 1.0, 6.0, ((0, 4), (1, 8))),
    }


def swap_blocks(blocks):
    row_count, block_count, full_width = blocks.shape
    viewed = blocks.reshape(row_count, block_count, block_count, full_width // block_count)
    return viewed.transpose(0, 2, 1, 3).reshape(row_count, block_count, full_width)


def gelu_exact(value):
    return 0.5 * value * (1.0 + jax.scipy.special.erf(value * 0.7071067811865476))


def gelu_slope(value):
    return 0.5 * (1.0 + jax.scipy.special.erf(value * 0.7071067811865476)) + value * jnp.exp(-0.5 * value * value) * 0.3989422804014327


def shard_pass(tokens_part, cotangent_part, up_in, up_out, down_in, down_out):
    row_count = tokens_part.shape[0]
    single = jnp.float32
    grid_in = tokens_part.reshape(row_count, NB, B)
    grid_grad = cotangent_part.reshape(row_count, NB, B)
    expanded = jnp.einsum('tjb,jbe->tje', grid_in.astype(single), up_in.astype(single)).astype(jnp.bfloat16)
    mixed_in = swap_blocks(expanded)
    before_act = jnp.einsum('tik,ike->tie', mixed_in.astype(single), up_out.astype(single))
    activated = gelu_exact(before_act).astype(jnp.bfloat16)
    reduced = jnp.einsum('tik,ike->tie', activated.astype(single), down_in.astype(single)).astype(jnp.bfloat16)
    mixed_out = swap_blocks(reduced)
    output = jnp.einsum('tjk,jbk->tjb', mixed_out.astype(single), down_out.astype(single)).astype(jnp.bfloat16)
    grad_mixed_out = jnp.einsum('tjb,jbk->tjk', grid_grad.astype(single), down_out.astype(single)).astype(jnp.bfloat16)
    grad_reduced = swap_blocks(grad_mixed_out)
    grad_act = jnp.einsum('tie,ike->tik', grad_reduced.astype(single), down_in.astype(single))
    grad_before = (grad_act * gelu_slope(before_act)).astype(jnp.bfloat16)
    grad_mixed_in = jnp.einsum('tie,ike->tik', grad_before.astype(single), up_out.astype(single)).astype(jnp.bfloat16)
    grad_expanded = swap_blocks(grad_mixed_in)
    input_grad = jnp.einsum('tje,jbe->tjb', grad_expanded.astype(single), up_in.astype(single)).astype(jnp.bfloat16)
    grad_up_in = jnp.einsum('tjb,tje->jbe', grid_in.astype(single), grad_expanded.astype(single))
    grad_up_out = jnp.einsum('tik,tie->ike', mixed_in.astype(single), grad_before.astype(single))
    grad_down_in = jnp.einsum('tik,tie->ike', activated.astype(single), grad_reduced.astype(single))
    grad_down_out = jnp.einsum('tjb,tjk->jbk', grid_grad.astype(single), mixed_out.astype(single))
    term = jnp.concatenate([grad_up_in, grad_up_out, grad_down_in, grad_down_out], axis=1).astype(jnp.bfloat16)
    term = lax.optimization_barrier(term)
    return output.reshape(row_count, D), input_grad.reshape(row_count, D), term.astype(jnp.float32)


def reference(tokens, up_in, up_out, down_in, down_out, cotangent):
    token_parts = tokens.reshape(N_SEQ, TOK_DEV, D)
    grad_parts = cotangent.reshape(N_SEQ, TOK_DEV, D)

    def accumulate(running, inputs):
        output, input_grad, term = shard_pass(inputs[0], inputs[1], up_in, up_out, down_in, down_out)
        return running + term, (output, input_grad)

    start_sum = jnp.zeros((NB, 2 * B + 2 * E, E), jnp.float32)
    running, (outputs, grads) = lax.scan(accumulate, start_sum, (token_parts, grad_parts))
    return outputs.reshape(TOKENS, D), grads.reshape(TOKENS, D), running
```

```python
import functools

import jax
import jax.numpy as jnp
from jax import lax
from jax.experimental import pallas as pl
from jax.experimental.pallas import tpu as pltpu
from jax.sharding import PartitionSpec as P

PARTS = (1, 1, 1, 1)
ORDER = (
    ("E0 M0 E1 F0 E2 M1", "T0 O0 M2 N0 E3 F1"),
    ("O1 M3 D0 F2 T1 I0", "I1 F3 T2 R0 N1 I2"),
    ("O2 I3 T3 R1 D1 N2", "O3 D2 N3 D3"),
)


PAIR = 2
VMEM = 62 * 1024 * 1024
SINGLE = jnp.float32
HALF = jnp.bfloat16


def dot(left, right, left_dim, right_dim):
    return lax.dot_general(
        left, right, (((left_dim,), (right_dim,)), ((), ())), preferred_element_type=SINGLE
    )


def params():
    return pltpu.CompilerParams(vmem_limit_bytes=VMEM)


def cost(*_):
    return pl.CostEstimate(flops=1024, bytes_accessed=1024, transcendentals=0)


def slot_of(order, parts, slot):
    return parts[0][order[slot], 0]


def part_specs(parts):
    line, _, rows, wide = parts[0].shape
    return [pl.BlockSpec((line, 1, rows, wide), lambda a, p: (0, a, 0, 0))]


def waits(after):
    return [pl.BlockSpec(memory_space=pl.ANY) for _ in after]


def expand_kernel(groups, count, flags, spots, *refs):
    shares, parts = refs[:groups], refs[groups : groups + count]
    own, send, weight = refs[-3:]
    line, blocks, width, block_width = weight.shape
    rows = own.shape[-2]
    piece = width // groups
    for n, share in enumerate(shares):
        place = pl.ds(pl.multiple_of(spots[n] * piece, piece), piece)
        for slot in range(line):
            for j in range(blocks):
                weight[slot, j, place, :] = share[spots[groups + slot], 0, j]
    for slot in range(line):
        here = slot_of(flags, parts, slot)
        for j in range(blocks):
            value = dot(
                weight[slot, j], here[:, j * block_width : (j + 1) * block_width], 1, 1
            ).astype(HALF)
            half = width // 2
            for i in range(blocks):
                own[0, i, slot, j] = value[i * rows : (i + 1) * rows]
                send[0, i, slot, j] = value[half + i * rows : half + (i + 1) * rows]


def expand(flags, spots, shares, parts, after):
    line, two, blocks, piece, block_width = shares[0].shape
    width = piece * len(shares)
    rows_here = parts[0].shape[-2]
    rows = width // (PAIR * blocks)
    shape = jax.ShapeDtypeStruct((two, blocks, line, blocks, rows, rows_here), HALF)
    out_spec = pl.BlockSpec((1,) + shape.shape[1:], lambda a, p, q: (a, 0, 0, 0, 0, 0))
    specs = [
        pl.BlockSpec(s.block_shape, lambda a, p, q, s=s: s.index_map(a, p)) for s in part_specs(parts)
    ]
    share_spec = pl.BlockSpec(
        (line, 1, blocks, piece, block_width), lambda a, p, q: (0, a, 0, 0, 0)
    )
    return pl.pallas_call(
        functools.partial(expand_kernel, len(shares), len(parts)),
        grid_spec=pltpu.PrefetchScalarGridSpec(
            num_scalar_prefetch=2,
            grid=(two,),
            in_specs=[share_spec] * len(shares) + specs + waits(after),
            out_specs=[out_spec, out_spec],
            scratch_shapes=[pltpu.VMEM((line, blocks, width, block_width), HALF)],
        ),
        out_shape=[shape, shape],
        compiler_params=params(),
        cost_estimate=cost(1),
        name="expand",
    )(flags, spots, *shares, *parts, *after)


def middle_kernel(places, own, recv, up, down, *refs):
    own_out, send_out, saved, result = refs[-4:]
    line, rows = own.shape[2], own.shape[3]

    def spot(half, slot):
        return pl.ds(pl.multiple_of(places[half * line + slot] * rows, rows), rows)

    for half, source in enumerate((own, recv)):
        for slot in range(line):
            saved[0, 0, 0, spot(half, slot), :] = source[0, 0, slot]
            saved[1, 1, 0, spot(half, slot), :] = source[1, 0, slot]
    before = dot(up[0], saved[0, 0, 0], 0, 0)
    bell = 0.5 * (1.0 + lax.erf(before * 0.7071067811865476))
    slope = bell + before * jnp.exp(-0.5 * before * before) * 0.3989422804014327
    saved[1, 0, 0] = (before * bell).astype(HALF)
    grad_act = dot(down[0], saved[1, 1, 0], 1, 0)
    saved[0, 1, 0] = (grad_act * slope).astype(HALF)
    result[0] = dot(up[0], saved[0, 1, 0], 1, 0).astype(HALF)
    result[1] = dot(down[0], saved[1, 0, 0], 0, 0).astype(HALF)
    for half, target in enumerate((own_out, send_out)):
        for slot in range(line):
            for a in range(2):
                target[a, 0, slot] = result[a, spot(half, slot), :]


def middle(places, own, recv, up, down, after):
    two, blocks, line, rows, rows_here = own.shape
    full = up.shape[1]
    part = pl.BlockSpec((two, 1, line, rows, rows_here), lambda i, p: (0, i, 0, 0, 0))
    factor = pl.BlockSpec((1, full, full), lambda i, p: (i, 0, 0))
    shape = jax.ShapeDtypeStruct(own.shape, HALF)
    kept = jax.ShapeDtypeStruct((2, 2, blocks, full, rows_here), HALF)
    return pl.pallas_call(
        middle_kernel,
        grid_spec=pltpu.PrefetchScalarGridSpec(
            num_scalar_prefetch=1,
            grid=(blocks,),
            in_specs=[part, part, factor, factor] + waits(after),
            out_specs=[
                part,
                part,
                pl.BlockSpec((2, 2, 1, full, rows_here), lambda i, p: (0, 0, i, 0, 0)),
            ],
            scratch_shapes=[pltpu.VMEM((2, full, rows_here), HALF)],
        ),
        out_shape=[shape, shape, kept],
        compiler_params=params(),
        cost_estimate=cost(8 * up.size * rows_here, own, recv, up, up, down, down, shape, shape, kept),
        name="middle",
    )(places, own, recv, up, down, *after)


def hidden(own, recv, a, slot, j):
    blocks, rows, rows_here = own.shape[1], own.shape[4], own.shape[5]
    return jnp.concatenate(
        [r[a, :, slot, j].reshape(blocks * rows, rows_here) for r in (own, recv)], axis=0
    )


def shrink_kernel(count, weight, own, recv, *rest):
    added, out, keep = rest[:count], rest[-2], rest[-1]
    blocks, block_width = weight.shape[2], weight.shape[-1]
    for j in range(blocks):
        at = slice(j * block_width, (j + 1) * block_width)
        value = dot(hidden(own, recv, 0, 0, j), weight[0, 0, j], 0, 0)
        for ref in added:
            value = value + ref[0, 0, :, at].astype(SINGLE)
        out[0, 0, :, at] = value.astype(HALF)
        if keep.shape == out.shape:
            keep[0, 0, :, at] = value.astype(HALF)
    if keep.shape != out.shape:
        keep[...] = jnp.zeros_like(keep)


def shrink(weight, own, recv, slots, added=(), after=(), twice=False):
    two, line, blocks, width, block_width = weight.shape
    rows, rows_here = own.shape[4:]
    first, count = slots
    shape = jax.ShapeDtypeStruct((count, two, rows_here, blocks * block_width), HALF)
    part = pl.BlockSpec(
        (1, blocks, 1, blocks, rows, rows_here), lambda s, a: (a, 0, s + first, 0, 0, 0)
    )

    def block(at):
        return pl.BlockSpec(
            (1, 1, rows_here, blocks * block_width), lambda s, a: (s + at, a, 0, 0)
        )

    return pl.pallas_call(
        functools.partial(shrink_kernel, len(added)),
        grid=(count, two),
        in_specs=[
            pl.BlockSpec((1, 1, blocks, width, block_width), lambda s, a: (a, s + first, 0, 0, 0)),
            part,
            part,
        ]
        + [block(at) for _, at in added]
        + waits(after),
        out_specs=[block(0), block(0) if twice else pl.BlockSpec((8, 128), lambda s, a: (0, 0))],
        out_shape=[shape, shape if twice else jax.ShapeDtypeStruct((8, 128), SINGLE)],
        compiler_params=params(),
        cost_estimate=cost(
            2 * count * weight.size // line * rows_here, shape, shape, *[shape for _ in added]
        ),
        name="shrink",
    )(weight, own, recv, *[a for a, _ in added], *after)


def join_kernel(left, right, *rest):
    out, token = rest[-2:]
    out[...] = left[...] + right[...]
    token[...] = jnp.zeros_like(token)


def join(left, right, after):
    spec = pl.BlockSpec((1,) + left.shape[1:], lambda s: (s, 0, 0, 0))
    return pl.pallas_call(
        join_kernel,
        grid=left.shape[:1],
        in_specs=[spec, spec] + waits(after),
        out_specs=[spec, pl.BlockSpec((8, 128), lambda s: (0, 0))],
        out_shape=[
            jax.ShapeDtypeStruct(left.shape, HALF),
            jax.ShapeDtypeStruct((8, 128), SINGLE),
        ],
        compiler_params=params(),
        cost_estimate=cost(1),
        name="join",
    )(left, right, *after)


def finish_kernel(weight, own, recv, passed, last, *rest):
    blocks, block_width = weight.shape[2], weight.shape[-1]
    for a, out in enumerate(rest[-2:]):
        for j in range(blocks):
            at = slice(j * block_width, (j + 1) * block_width)
            value = dot(hidden(own, recv, a, 0, j), weight[a, 0, j], 0, 0)
            value = value + passed[0, a, :, at].astype(SINGLE) + last[0, a, :, at].astype(SINGLE)
            out[:, at] = value.astype(HALF)


def finish(weight, own, recv, passed, last, rows_all, at, before, after):
    two, line, blocks, width, block_width = weight.shape
    rows, rows_here = own.shape[4:]
    wide = blocks * block_width
    shape = jax.ShapeDtypeStruct((rows_all, wide), HALF)
    part = pl.BlockSpec((two, blocks, 1, blocks, rows, rows_here), lambda s: (0, 0, 0, 0, 0, 0))
    block = pl.BlockSpec((1, two, rows_here, wide), lambda s: (0, 0, 0, 0))
    out_spec = pl.BlockSpec((rows_here, wide), lambda s: (at, 0))
    return pl.pallas_call(
        finish_kernel,
        grid=(1,),
        in_specs=[
            pl.BlockSpec((two, 1, blocks, width, block_width), lambda s: (0, 0, 0, 0, 0)),
            part,
            part,
            block,
            block,
        ]
        + waits(before)
        + waits(after),
        out_specs=[out_spec, out_spec],
        out_shape=[shape, shape],
        input_output_aliases={5: 0, 6: 1} if before else {},
        compiler_params=params(),
        cost_estimate=cost(2 * weight.size // line * rows_here, passed, last),
        name="finish",
    )(weight, own, recv, passed, last, *before, *after)


def outer_kernel(count, more, flags, own, recv, *refs):
    parts, before = refs[:count], refs[count : count + more]
    out, token = refs[-2:]
    line, blocks, _, block_width = out.shape[1:]
    token[...] = jnp.zeros_like(token)
    for slot in range(line):
        here = slot_of(flags, parts, slot)
        for j in range(blocks):
            value = dot(
                hidden(own, recv, 0, slot, j),
                here[:, j * block_width : (j + 1) * block_width],
                1,
                0,
            )
            for ref in before:
                value = value + ref[0, slot, j]
            out[0, slot, j] = value


def outer(flags, weight, own, recv, parts, before, after):
    rows_here = own.shape[5]
    part = pl.BlockSpec((1,) + own.shape[1:], lambda a, p: (a, 0, 0, 0, 0, 0))
    shape = jax.ShapeDtypeStruct(weight.shape, SINGLE)
    total = pl.BlockSpec((1,) + weight.shape[1:], lambda a, p: (a, 0, 0, 0, 0))
    return pl.pallas_call(
        functools.partial(outer_kernel, len(parts), len(before)),
        grid_spec=pltpu.PrefetchScalarGridSpec(
            num_scalar_prefetch=1,
            grid=(weight.shape[0],),
            in_specs=[part, part]
            + part_specs(parts)
            + [total for _ in before]
            + waits(after),
            out_specs=[total, pl.BlockSpec((8, 128), lambda a, p: (0, 0))],
        ),
        out_shape=[shape, jax.ShapeDtypeStruct((8, 128), SINGLE)],
        input_output_aliases={3 + len(parts): 0} if before else {},
        compiler_params=params(),
        cost_estimate=cost(2 * weight.size * rows_here, own, recv, *parts, shape, shape),
        name="outer",
    )(flags, own, recv, *parts, *before, *after)


def inner_kernel(count, *refs):
    saved, out = refs[: 2 * count], refs[-1]
    m = pl.program_id(0)
    last = pl.num_programs(0) - 1
    edge = (m == 0) | (m == last)

    @pl.when(edge)
    def _():
        out[...] = jnp.zeros_like(out)

    @pl.when(jnp.logical_not(edge))
    def _():
        value, held = 0.0, []
        for left, right in zip(saved[::2], saved[1::2]):
            held.append((left[0, 0, 0], right[0, 0, 0]))
            if sum(h[0].shape[1] for h in held) >= 256:
                left, right = (jnp.concatenate(v, axis=1) for v in zip(*held))
                value, held = value + dot(left, right, 1, 1), []
        out[0] = value.astype(HALF)


def inner(saved, block_width, i, first, held, before, after):
    _, _, blocks, full, _ = saved[0].shape
    per = full // block_width
    steps = 2 * per + 2

    def at(m):
        row = jnp.clip(m - 1, 0, 2 * per - 1)
        return row // per, row % per

    specs = []
    for s in saved:
        left = (1, 1, 1, block_width, s.shape[-1])
        right = (1, 1, 1, full, s.shape[-1])
        specs.append(pl.BlockSpec(left, lambda m: (at(m)[0], 0, i, at(m)[1], 0)))
        specs.append(pl.BlockSpec(right, lambda m: (at(m)[0], 1, i, 0, 0)))
    return pl.pallas_call(
        functools.partial(inner_kernel, len(saved)),
        grid=(steps,),
        in_specs=specs + waits(before) + waits(after),
        out_specs=pl.BlockSpec((1, block_width, full), lambda m: (i - first, m, 0)),
        out_shape=jax.ShapeDtypeStruct((held, steps * block_width, full), HALF),
        input_output_aliases={2 * len(saved): 0} if before else {},
        compiler_params=params(),
        cost_estimate=cost(1),
        name="inner",
    )(*[s for s in saved for _ in range(2)], *before, *after)


def assemble_kernel(edges, summed, kept, *rest):
    out = rest[-1]
    width = kept.shape[1]
    out[...] = summed[...].astype(SINGLE)

    @pl.when(edges[0] == 1)
    def _():
        out[:, :width] = kept[...].astype(SINGLE)

    @pl.when(edges[1] == 1)
    def _():
        out[:, out.shape[1] - width :] = kept[...].astype(SINGLE)


def assemble(edges, summed, kept, first, blocks, before):
    held, rows, full = summed.shape
    wide = 256
    spec = pl.BlockSpec((1, rows, wide), lambda i, c, p: (i, 0, c))
    return pl.pallas_call(
        assemble_kernel,
        grid_spec=pltpu.PrefetchScalarGridSpec(
            num_scalar_prefetch=1,
            grid=(held, full // wide),
            in_specs=[
                spec,
                pl.BlockSpec((1, kept.shape[1], wide), lambda i, c, p: (i + first, 0, c)),
            ]
            + waits(before),
            out_specs=pl.BlockSpec((1, rows, wide), lambda i, c, p: (i + first, 0, c)),
        ),
        out_shape=jax.ShapeDtypeStruct((blocks, rows, full), SINGLE),
        input_output_aliases={3: 0} if before else {},
        compiler_params=params(),
        cost_estimate=cost(1),
        name="assemble",
    )(edges, summed, kept, *before)


def on_device(tokens, up_in, up_out, down_in, down_out, cotangent):
    rows_all = tokens.shape[0]
    blocks, block_width, full = up_in.shape
    peers, groups = lax.axis_size("blk"), lax.axis_size("seq")
    line = peers // PAIR
    piece = full // (blocks * peers)
    width = PAIR * blocks * piece
    rows = blocks * piece
    at_line, at_pair = lax.axis_index("blk") // PAIR, lax.axis_index("blk") % PAIR
    at_group = lax.axis_index("seq")
    along = [[o * PAIR + q for o in range(line)] for q in range(PAIR)]
    parts = PARTS
    sizes = [rows_all * k // sum(parts) for k in parts]
    starts = [sum(sizes[:c]) for c in range(len(sizes))]
    count = len(sizes)
    short = line == 4

    def lines(pairs):
        return [(a * PAIR + q, b * PAIR + q) for a, b in pairs for q in range(PAIR)]

    def hop(value, pairs):
        return lax.ppermute(value, "blk", lines(pairs))

    def other(value):
        return lax.ppermute(value, "blk", [(k, k ^ 1) for k in range(peers)])

    ends, turn = [(0, 1), (1, 0), (2, 3), (3, 2)], [(1, 2), (2, 1)]
    inward = [(0, 1), (3, 2)]
    if short:
        order = jnp.array([[0, 1, 2, 3], [1, 0, 2, 3], [2, 3, 1, 0], [3, 2, 1, 0]], jnp.int32)[
            at_line
        ]
    else:
        order = jnp.arange(line, dtype=jnp.int32)
    flags = order
    places = jnp.concatenate([order * PAIR + at_pair, order * PAIR + 1 - at_pair])

    def across(pieces):
        if not short:
            moved = lax.all_to_all(pieces, "blk", 0, 0, axis_index_groups=along, tiled=True)
            return jnp.take(moved, (at_line - jnp.arange(line)) % line, axis=0)
        moved = []
        for far in range(line):
            piece_at = lax.dynamic_index_in_dim(pieces, (at_line + far) % line, 0, keepdims=False)
            moved.append(hop(piece_at, [(k, (k + far) % line) for k in range(line)]) if far else piece_at)
        return jnp.stack(moved)

    chunks = [jnp.stack([v[k : k + n] for v in (tokens, cotangent)]) for k, n in zip(starts, sizes)]

    def step_gather(c, at):
        mine = chunks[c]
        if shared["total"] and not short:
            mine, _ = lax.optimization_barrier((mine, shared["total"][0]))
        at["parts"] = [lax.all_gather(mine, "blk", axis_index_groups=along)]

    factors = jnp.stack([up_in, down_out]).reshape(
        2, blocks, block_width, line, groups, width // groups
    )
    share = lax.dynamic_index_in_dim(factors, at_group, 4, keepdims=False)
    share = across(share.transpose(3, 0, 1, 4, 2))
    shares = [share, lax.ppermute(share, "seq", [(k, k ^ 2) for k in range(groups)])]
    shares += [lax.ppermute(v, "seq", [(k, k ^ 1) for k in range(groups)]) for v in shares]
    whose = at_group ^ jnp.array([0, 2, 1, 3], jnp.int32)
    stand = (whose + at_pair * (groups // 2)) % groups
    source = (at_line - order) % line
    spots = jnp.concatenate([stand, source]).astype(jnp.int32)
    def whole_weight(first):
        held, _ = lax.optimization_barrier((tuple(shares), first))
        held = jnp.stack(held)[jnp.argsort(stand)][:, source]
        held = held.transpose(2, 1, 3, 0, 4, 5)
        return held.reshape(2, line, blocks, width, block_width)

    flat = (2, blocks, line, rows, -1)
    deep = (2, blocks, line, blocks, piece, -1)
    state = [dict() for _ in range(count)]
    terms, summed = [], []
    shared = {"after": (), "results": (), "total": (), "inner": ()}

    def step_expand(c, at):
        at["own"], send = expand(flags, spots, shares, at["parts"], shared["after"])
        at["recv"] = other(send)
        shared["after"] = (at["own"],)
        if c == 0:
            shared["weight"] = whole_weight(at["own"])

    def step_middle(c, at):
        own, send, at["saved"] = middle(
            places,
            at["own"].reshape(flat),
            at["recv"].reshape(flat),
            up_out,
            down_in,
            shared["after"] + ((shared["weight"],) if c == 0 else ()),
        )
        at["own"], at["recv"] = own.reshape(deep), other(send).reshape(deep)
        shared["after"] = (own,)

    def step_far(c, at):
        sent, at["sum"] = shrink(
            shared["weight"], at["own"], at["recv"], (2, 2), (), shared["after"], twice=True
        )
        at["arrived"] = hop(sent, inward)
        shared["after"] = (at["sum"],)

    def step_turn(c, at):
        both, token = join(at["sum"], at["arrived"], shared["after"])
        at["passed"] = hop(both, turn)
        shared["after"] = (token,)

    def step_near(c, at):
        near, kept = shrink(
            shared["weight"], at["own"], at["recv"], (1, 1), [(at["passed"], 1)], shared["after"]
        )
        at["last"] = hop(near, ends)
        shared["after"] = (kept,)

    def step_finish(c, at):
        shared["results"] = finish(
            shared["weight"],
            at["own"],
            at["recv"],
            at["passed"],
            at["last"],
            rows_all,
            starts[c] // sizes[c],
            shared["results"],
            shared["after"],
        )
        shared["after"] = shared["after"] + (at["last"],)

    def step_whole(c, at):
        result, kept = shrink(
            shared["weight"], at["own"], at["recv"], (0, line), (), shared["after"]
        )
        at["result"] = lax.psum_scatter(
            result, "blk", scatter_dimension=0, axis_index_groups=along
        )
        shared["after"] = (kept,)

    def step_outer(c, at):
        total, token = outer(
            flags, shared["weight"], at["own"], at["recv"], at["parts"], shared["total"], shared["after"]
        )
        shared["total"], shared["after"] = (total,), (token,)

    held = max(blocks // 2, 1)

    def step_inner(i, at):
        kept = [s["saved"] for s in state]
        first = i // held * held
        before = shared["inner"] if i > first else ()
        done = inner(kept, block_width, i, first, held, before, shared["after"])
        shared["inner"] = (done,)
        if i == first + held - 1:
            terms.append(done)

    def step_reduce(h, at):
        term, _ = lax.optimization_barrier((terms[h], shared["after"][0]))
        summed.append(lax.psum_scatter(term, "seq", scatter_dimension=1, tiled=True))

    steps = dict(
        G=step_gather, E=step_expand, M=step_middle, F=step_far, T=step_turn,
        N=step_near, D=step_finish, W=step_whole, O=step_outer, I=step_inner, R=step_reduce,
    )
    if short:
        plan = [("G", c) for c in range(count)]
        plan += [(w[0], int(w[1:])) for row in ORDER for half in row for w in half.split()]
    else:
        plan = [(k, c) for c in range(count) for k in "GEMWO"] + [("I", i) for i in range(blocks)]
        plan += [("R", h) for h in range(blocks // held)]
    for name, c in plan:
        steps[name](c, state[c] if c < count else None)
    total = shared["total"][0].astype(HALF)
    first = at_group % 2 == 0
    sent = jnp.where(first, total[1], total[0])
    kept = jnp.where(first, total[0], total[1]).astype(SINGLE)
    kept = kept + lax.ppermute(sent, "seq", [(k, k ^ 1) for k in range(groups)]).astype(SINGLE)
    kept = kept + lax.ppermute(kept.astype(HALF), "seq", [(2, 0), (1, 3)]).astype(SINGLE)
    kept = jnp.where(at_pair == 0, kept, jnp.roll(kept, width // 2, axis=2)).astype(HALF)
    kept = across(jnp.take(kept, jnp.argsort(order), axis=0))
    kept = jnp.take(kept, (at_line - jnp.arange(line)) % line, axis=0)
    kept = kept.transpose(1, 3, 0, 2).reshape(blocks, block_width, full)
    edges = jnp.stack([at_group == 0, at_group == groups - 1]).astype(jnp.int32)
    weight_grads = ()
    for first, part in enumerate(summed):
        weight_grads = (assemble(edges, part, kept, first * held, blocks, weight_grads),)
    weight_grads = weight_grads[0]
    if short:
        grad, result = shared["results"]
    else:
        result = jnp.concatenate([s["result"] for s in state], axis=1)
        grad, result = result[0], result[1]
    return result, grad, weight_grads


def solution(mesh):
    placed = (
        P("seq", "blk"),
        P("blk", None, None),
        P("blk", None, None),
        P("blk", None, None),
        P("blk", None, None),
        P("seq", "blk"),
    )
    return jax.shard_map(
        on_device,
        mesh=mesh,
        in_specs=placed,
        out_specs=(P("seq", "blk"), P("seq", "blk"), P("blk", "seq", None)),
        check_vma=False,
    )
```

```python
import functools

import jax
import jax.numpy as jnp
from jax import lax
from jax.experimental import pallas as pl
from jax.experimental.pallas import tpu as pltpu
from jax.sharding import PartitionSpec as P

PARTS = (1, 1, 1, 1)
ORDER = (
    ("E0 M0 E1", "F0 E2 M1", "T0 O0 M2", "N0 E3 F1"),
    ("O1 M3 D0", "F2 T1 I0", "I1 F3 R0", "N1 T2 O2"),
    ("O3 I2 I3", "N2 T3 R1", "D1 N3 D2 D3"),
)


PAIR = 2
VMEM = 62 * 1024 * 1024
SINGLE = jnp.float32
HALF = jnp.bfloat16


def dot(left, right, left_dim, right_dim):
    return lax.dot_general(
        left, right, (((left_dim,), (right_dim,)), ((), ())), preferred_element_type=SINGLE
    )


def params():
    return pltpu.CompilerParams(vmem_limit_bytes=VMEM)


def cost(*_):
    return pl.CostEstimate(flops=1024, bytes_accessed=1024, transcendentals=0)


def slot_of(order, parts, slot):
    return parts[0][order[slot], 0]


def part_specs(parts):
    line, _, rows, wide = parts[0].shape
    return [pl.BlockSpec((line, 1, rows, wide), lambda a, p: (0, a, 0, 0))]


def waits(after):
    return [pl.BlockSpec(memory_space=pl.ANY) for _ in after]


def expand_kernel(groups, count, flags, spots, *refs):
    shares, parts = refs[:groups], refs[groups : groups + count]
    own, send, weight = refs[-3:]
    line, blocks, width, block_width = weight.shape
    rows = own.shape[-2]
    piece = width // groups
    for n, share in enumerate(shares):
        place = pl.ds(pl.multiple_of(spots[n] * piece, piece), piece)
        for slot in range(line):
            for j in range(blocks):
                weight[slot, j, place, :] = share[spots[groups + slot], 0, j]
    for slot in range(line):
        here = slot_of(flags, parts, slot)
        for j in range(blocks):
            value = dot(
                weight[slot, j], here[:, j * block_width : (j + 1) * block_width], 1, 1
            ).astype(HALF)
            half = width // 2
            for i in range(blocks):
                own[0, i, slot, j] = value[i * rows : (i + 1) * rows]
                send[0, i, slot, j] = value[half + i * rows : half + (i + 1) * rows]


def expand(flags, spots, shares, parts, after):
    line, two, blocks, piece, block_width = shares[0].shape
    width = piece * len(shares)
    rows_here = parts[0].shape[-2]
    rows = width // (PAIR * blocks)
    shape = jax.ShapeDtypeStruct((two, blocks, line, blocks, rows, rows_here), HALF)
    out_spec = pl.BlockSpec((1,) + shape.shape[1:], lambda a, p, q: (a, 0, 0, 0, 0, 0))
    specs = [
        pl.BlockSpec(s.block_shape, lambda a, p, q, s=s: s.index_map(a, p)) for s in part_specs(parts)
    ]
    share_spec = pl.BlockSpec(
        (line, 1, blocks, piece, block_width), lambda a, p, q: (0, a, 0, 0, 0)
    )
    return pl.pallas_call(
        functools.partial(expand_kernel, len(shares), len(parts)),
        grid_spec=pltpu.PrefetchScalarGridSpec(
            num_scalar_prefetch=2,
            grid=(two,),
            in_specs=[share_spec] * len(shares) + specs + waits(after),
            out_specs=[out_spec, out_spec],
            scratch_shapes=[pltpu.VMEM((line, blocks, width, block_width), HALF)],
        ),
        out_shape=[shape, shape],
        compiler_params=params(),
        cost_estimate=cost(1),
        name="expand",
    )(flags, spots, *shares, *parts, *after)


def middle_kernel(places, own, recv, up, down, *refs):
    own_out, send_out, saved, result = refs[-4:]
    line, rows = own.shape[2], own.shape[3]

    def spot(half, slot):
        return pl.ds(pl.multiple_of(places[half * line + slot] * rows, rows), rows)

    for half, source in enumerate((own, recv)):
        for slot in range(line):
            saved[0, 0, 0, spot(half, slot), :] = source[0, 0, slot]
            saved[1, 1, 0, spot(half, slot), :] = source[1, 0, slot]
    before = dot(up[0], saved[0, 0, 0], 0, 0)
    bell = 0.5 * (1.0 + lax.erf(before * 0.7071067811865476))
    slope = bell + before * jnp.exp(-0.5 * before * before) * 0.3989422804014327
    saved[1, 0, 0] = (before * bell).astype(HALF)
    grad_act = dot(down[0], saved[1, 1, 0], 1, 0)
    saved[0, 1, 0] = (grad_act * slope).astype(HALF)
    result[0] = dot(up[0], saved[0, 1, 0], 1, 0).astype(HALF)
    result[1] = dot(down[0], saved[1, 0, 0], 0, 0).astype(HALF)
    for half, target in enumerate((own_out, send_out)):
        for slot in range(line):
            for a in range(2):
                target[a, 0, slot] = result[a, spot(half, slot), :]


def middle(places, own, recv, up, down, after):
    two, blocks, line, rows, rows_here = own.shape
    full = up.shape[1]
    part = pl.BlockSpec((two, 1, line, rows, rows_here), lambda i, p: (0, i, 0, 0, 0))
    factor = pl.BlockSpec((1, full, full), lambda i, p: (i, 0, 0))
    shape = jax.ShapeDtypeStruct(own.shape, HALF)
    kept = jax.ShapeDtypeStruct((2, 2, blocks, full, rows_here), HALF)
    return pl.pallas_call(
        middle_kernel,
        grid_spec=pltpu.PrefetchScalarGridSpec(
            num_scalar_prefetch=1,
            grid=(blocks,),
            in_specs=[part, part, factor, factor] + waits(after),
            out_specs=[
                part,
                part,
                pl.BlockSpec((2, 2, 1, full, rows_here), lambda i, p: (0, 0, i, 0, 0)),
            ],
            scratch_shapes=[pltpu.VMEM((2, full, rows_here), HALF)],
        ),
        out_shape=[shape, shape, kept],
        compiler_params=params(),
        cost_estimate=cost(8 * up.size * rows_here, own, recv, up, up, down, down, shape, shape, kept),
        name="middle",
    )(places, own, recv, up, down, *after)


def hidden(own, recv, a, slot, j):
    blocks, rows, rows_here = own.shape[1], own.shape[4], own.shape[5]
    return jnp.concatenate(
        [r[a, :, slot, j].reshape(blocks * rows, rows_here) for r in (own, recv)], axis=0
    )


def shrink_kernel(count, weight, own, recv, *rest):
    added, out, keep = rest[:count], rest[-2], rest[-1]
    blocks, block_width = weight.shape[2], weight.shape[-1]
    for j in range(blocks):
        at = slice(j * block_width, (j + 1) * block_width)
        value = dot(hidden(own, recv, 0, 0, j), weight[0, 0, j], 0, 0)
        for ref in added:
            value = value + ref[0, 0, :, at].astype(SINGLE)
        out[0, 0, :, at] = value.astype(HALF)
        if keep.shape == out.shape:
            keep[0, 0, :, at] = value.astype(HALF)
    if keep.shape != out.shape:
        keep[...] = jnp.zeros_like(keep)


def shrink(weight, own, recv, slots, added=(), after=(), twice=False):
    two, line, blocks, width, block_width = weight.shape
    rows, rows_here = own.shape[4:]
    first, count = slots
    shape = jax.ShapeDtypeStruct((count, two, rows_here, blocks * block_width), HALF)
    part = pl.BlockSpec(
        (1, blocks, 1, blocks, rows, rows_here), lambda s, a: (a, 0, s + first, 0, 0, 0)
    )

    def block(at):
        return pl.BlockSpec(
            (1, 1, rows_here, blocks * block_width), lambda s, a: (s + at, a, 0, 0)
        )

    return pl.pallas_call(
        functools.partial(shrink_kernel, len(added)),
        grid=(count, two),
        in_specs=[
            pl.BlockSpec((1, 1, blocks, width, block_width), lambda s, a: (a, s + first, 0, 0, 0)),
            part,
            part,
        ]
        + [block(at) for _, at in added]
        + waits(after),
        out_specs=[block(0), block(0) if twice else pl.BlockSpec((8, 128), lambda s, a: (0, 0))],
        out_shape=[shape, shape if twice else jax.ShapeDtypeStruct((8, 128), SINGLE)],
        compiler_params=params(),
        cost_estimate=cost(
            2 * count * weight.size // line * rows_here, shape, shape, *[shape for _ in added]
        ),
        name="shrink",
    )(weight, own, recv, *[a for a, _ in added], *after)


def join_kernel(left, right, *rest):
    out, token = rest[-2:]
    out[...] = left[...] + right[...]
    token[...] = jnp.zeros_like(token)


def join(left, right, after):
    spec = pl.BlockSpec((1,) + left.shape[1:], lambda s: (s, 0, 0, 0))
    return pl.pallas_call(
        join_kernel,
        grid=left.shape[:1],
        in_specs=[spec, spec] + waits(after),
        out_specs=[spec, pl.BlockSpec((8, 128), lambda s: (0, 0))],
        out_shape=[
            jax.ShapeDtypeStruct(left.shape, HALF),
            jax.ShapeDtypeStruct((8, 128), SINGLE),
        ],
        compiler_params=params(),
        cost_estimate=cost(1),
        name="join",
    )(left, right, *after)


def finish_kernel(weight, own, recv, passed, last, *rest):
    blocks, block_width = weight.shape[2], weight.shape[-1]
    for a, out in enumerate(rest[-2:]):
        for j in range(blocks):
            at = slice(j * block_width, (j + 1) * block_width)
            value = dot(hidden(own, recv, a, 0, j), weight[a, 0, j], 0, 0)
            value = value + passed[0, a, :, at].astype(SINGLE) + last[0, a, :, at].astype(SINGLE)
            out[:, at] = value.astype(HALF)


def finish(weight, own, recv, passed, last, rows_all, at, before, after):
    two, line, blocks, width, block_width = weight.shape
    rows, rows_here = own.shape[4:]
    wide = blocks * block_width
    shape = jax.ShapeDtypeStruct((rows_all, wide), HALF)
    part = pl.BlockSpec((two, blocks, 1, blocks, rows, rows_here), lambda s: (0, 0, 0, 0, 0, 0))
    block = pl.BlockSpec((1, two, rows_here, wide), lambda s: (0, 0, 0, 0))
    out_spec = pl.BlockSpec((rows_here, wide), lambda s: (at, 0))
    return pl.pallas_call(
        finish_kernel,
        grid=(1,),
        in_specs=[
            pl.BlockSpec((two, 1, blocks, width, block_width), lambda s: (0, 0, 0, 0, 0)),
            part,
            part,
            block,
            block,
        ]
        + waits(before)
        + waits(after),
        out_specs=[out_spec, out_spec],
        out_shape=[shape, shape],
        input_output_aliases={5: 0, 6: 1} if before else {},
        compiler_params=params(),
        cost_estimate=cost(2 * weight.size // line * rows_here, passed, last),
        name="finish",
    )(weight, own, recv, passed, last, *before, *after)


def outer_kernel(count, more, flags, own, recv, *refs):
    parts, before = refs[:count], refs[count : count + more]
    out, token = refs[-2:]
    line, blocks, _, block_width = out.shape[1:]
    token[...] = jnp.zeros_like(token)
    for slot in range(line):
        here = slot_of(flags, parts, slot)
        for j in range(blocks):
            value = dot(
                hidden(own, recv, 0, slot, j),
                here[:, j * block_width : (j + 1) * block_width],
                1,
                0,
            )
            for ref in before:
                value = value + ref[0, slot, j]
            out[0, slot, j] = value


def outer(flags, weight, own, recv, parts, before, after):
    rows_here = own.shape[5]
    part = pl.BlockSpec((1,) + own.shape[1:], lambda a, p: (a, 0, 0, 0, 0, 0))
    shape = jax.ShapeDtypeStruct(weight.shape, SINGLE)
    total = pl.BlockSpec((1,) + weight.shape[1:], lambda a, p: (a, 0, 0, 0, 0))
    return pl.pallas_call(
        functools.partial(outer_kernel, len(parts), len(before)),
        grid_spec=pltpu.PrefetchScalarGridSpec(
            num_scalar_prefetch=1,
            grid=(weight.shape[0],),
            in_specs=[part, part]
            + part_specs(parts)
            + [total for _ in before]
            + waits(after),
            out_specs=[total, pl.BlockSpec((8, 128), lambda a, p: (0, 0))],
        ),
        out_shape=[shape, jax.ShapeDtypeStruct((8, 128), SINGLE)],
        input_output_aliases={3 + len(parts): 0} if before else {},
        compiler_params=params(),
        cost_estimate=cost(2 * weight.size * rows_here, own, recv, *parts, shape, shape),
        name="outer",
    )(flags, own, recv, *parts, *before, *after)


def inner_kernel(count, *refs):
    saved, out = refs[: 2 * count], refs[-1]
    m = pl.program_id(0)
    last = pl.num_programs(0) - 1
    edge = (m == 0) | (m == last)

    @pl.when(edge)
    def _():
        out[...] = jnp.zeros_like(out)

    @pl.when(jnp.logical_not(edge))
    def _():
        value, held = 0.0, []
        for left, right in zip(saved[::2], saved[1::2]):
            held.append((left[0, 0, 0], right[0, 0, 0]))
            if sum(h[0].shape[1] for h in held) >= 256:
                left, right = (jnp.concatenate(v, axis=1) for v in zip(*held))
                value, held = value + dot(left, right, 1, 1), []
        out[0] = value.astype(HALF)


def inner(saved, block_width, i, first, held, before, after):
    _, _, blocks, full, _ = saved[0].shape
    per = full // block_width
    steps = 2 * per + 2

    def at(m):
        row = jnp.clip(m - 1, 0, 2 * per - 1)
        return row // per, row % per

    specs = []
    for s in saved:
        left = (1, 1, 1, block_width, s.shape[-1])
        right = (1, 1, 1, full, s.shape[-1])
        specs.append(pl.BlockSpec(left, lambda m: (at(m)[0], 0, i, at(m)[1], 0)))
        specs.append(pl.BlockSpec(right, lambda m: (at(m)[0], 1, i, 0, 0)))
    return pl.pallas_call(
        functools.partial(inner_kernel, len(saved)),
        grid=(steps,),
        in_specs=specs + waits(before) + waits(after),
        out_specs=pl.BlockSpec((1, block_width, full), lambda m: (i - first, m, 0)),
        out_shape=jax.ShapeDtypeStruct((held, steps * block_width, full), HALF),
        input_output_aliases={2 * len(saved): 0} if before else {},
        compiler_params=params(),
        cost_estimate=cost(1),
        name="inner",
    )(*[s for s in saved for _ in range(2)], *before, *after)


def assemble_kernel(edges, summed, kept, *rest):
    out = rest[-1]
    width = kept.shape[1]
    out[...] = summed[...].astype(SINGLE)

    @pl.when(edges[0] == 1)
    def _():
        out[:, :width] = kept[...].astype(SINGLE)

    @pl.when(edges[1] == 1)
    def _():
        out[:, out.shape[1] - width :] = kept[...].astype(SINGLE)


def assemble(edges, summed, kept, first, blocks, before):
    held, rows, full = summed.shape
    wide = 256
    spec = pl.BlockSpec((1, rows, wide), lambda i, c, p: (i, 0, c))
    return pl.pallas_call(
        assemble_kernel,
        grid_spec=pltpu.PrefetchScalarGridSpec(
            num_scalar_prefetch=1,
            grid=(held, full // wide),
            in_specs=[
                spec,
                pl.BlockSpec((1, kept.shape[1], wide), lambda i, c, p: (i + first, 0, c)),
            ]
            + waits(before),
            out_specs=pl.BlockSpec((1, rows, wide), lambda i, c, p: (i + first, 0, c)),
        ),
        out_shape=jax.ShapeDtypeStruct((blocks, rows, full), SINGLE),
        input_output_aliases={3: 0} if before else {},
        compiler_params=params(),
        cost_estimate=cost(1),
        name="assemble",
    )(edges, summed, kept, *before)


def on_device(tokens, up_in, up_out, down_in, down_out, cotangent):
    rows_all = tokens.shape[0]
    blocks, block_width, full = up_in.shape
    peers, groups = lax.axis_size("blk"), lax.axis_size("seq")
    line = peers // PAIR
    piece = full // (blocks * peers)
    width = PAIR * blocks * piece
    rows = blocks * piece
    at_line, at_pair = lax.axis_index("blk") // PAIR, lax.axis_index("blk") % PAIR
    at_group = lax.axis_index("seq")
    along = [[o * PAIR + q for o in range(line)] for q in range(PAIR)]
    parts = PARTS
    sizes = [rows_all * k // sum(parts) for k in parts]
    starts = [sum(sizes[:c]) for c in range(len(sizes))]
    count = len(sizes)
    short = line == 4

    def lines(pairs):
        return [(a * PAIR + q, b * PAIR + q) for a, b in pairs for q in range(PAIR)]

    def hop(value, pairs):
        return lax.ppermute(value, "blk", lines(pairs))

    def other(value):
        return lax.ppermute(value, "blk", [(k, k ^ 1) for k in range(peers)])

    ends, turn = [(0, 1), (1, 0), (2, 3), (3, 2)], [(1, 2), (2, 1)]
    inward = [(0, 1), (3, 2)]
    if short:
        order = jnp.array([[0, 1, 2, 3], [1, 0, 2, 3], [2, 3, 1, 0], [3, 2, 1, 0]], jnp.int32)[
            at_line
        ]
    else:
        order = jnp.arange(line, dtype=jnp.int32)
    flags = order
    places = jnp.concatenate([order * PAIR + at_pair, order * PAIR + 1 - at_pair])

    def across(pieces):
        if not short:
            moved = lax.all_to_all(pieces, "blk", 0, 0, axis_index_groups=along, tiled=True)
            return jnp.take(moved, (at_line - jnp.arange(line)) % line, axis=0)
        moved = []
        for far in range(line):
            piece_at = lax.dynamic_index_in_dim(pieces, (at_line + far) % line, 0, keepdims=False)
            moved.append(hop(piece_at, [(k, (k + far) % line) for k in range(line)]) if far else piece_at)
        return jnp.stack(moved)

    chunks = [jnp.stack([v[k : k + n] for v in (tokens, cotangent)]) for k, n in zip(starts, sizes)]

    def step_gather(c, at):
        mine = chunks[c]
        if shared["total"] and not short:
            mine, _ = lax.optimization_barrier((mine, shared["total"][0]))
        at["parts"] = [lax.all_gather(mine, "blk", axis_index_groups=along)]

    factors = jnp.stack([up_in, down_out]).reshape(
        2, blocks, block_width, line, groups, width // groups
    )
    share = lax.dynamic_index_in_dim(factors, at_group, 4, keepdims=False)
    share = across(share.transpose(3, 0, 1, 4, 2))
    shares = [share, lax.ppermute(share, "seq", [(k, k ^ 2) for k in range(groups)])]
    shares += [lax.ppermute(v, "seq", [(k, k ^ 1) for k in range(groups)]) for v in shares]
    whose = at_group ^ jnp.array([0, 2, 1, 3], jnp.int32)
    stand = (whose + at_pair * (groups // 2)) % groups
    source = (at_line - order) % line
    spots = jnp.concatenate([stand, source]).astype(jnp.int32)
    def whole_weight(first):
        held, _ = lax.optimization_barrier((tuple(shares), first))
        held = jnp.stack(held)[jnp.argsort(stand)][:, source]
        held = held.transpose(2, 1, 3, 0, 4, 5)
        return held.reshape(2, line, blocks, width, block_width)

    flat = (2, blocks, line, rows, -1)
    deep = (2, blocks, line, blocks, piece, -1)
    state = [dict() for _ in range(count)]
    terms, summed = [], []
    shared = {"after": (), "results": (), "total": (), "inner": ()}

    def step_expand(c, at):
        at["own"], send = expand(flags, spots, shares, at["parts"], shared["after"])
        at["recv"] = other(send)
        shared["after"] = (at["own"],)
        if c == 0:
            shared["weight"] = whole_weight(at["own"])

    def step_middle(c, at):
        own, send, at["saved"] = middle(
            places,
            at["own"].reshape(flat),
            at["recv"].reshape(flat),
            up_out,
            down_in,
            shared["after"] + ((shared["weight"],) if c == 0 else ()),
        )
        at["own"], at["recv"] = own.reshape(deep), other(send).reshape(deep)
        shared["after"] = (own,)

    def step_far(c, at):
        sent, at["sum"] = shrink(
            shared["weight"], at["own"], at["recv"], (2, 2), (), shared["after"], twice=True
        )
        at["arrived"] = hop(sent, inward)
        shared["after"] = (at["sum"],)

    def step_turn(c, at):
        both, token = join(at["sum"], at["arrived"], shared["after"])
        at["passed"] = hop(both, turn)
        shared["after"] = (token,)

    def step_near(c, at):
        near, kept = shrink(
            shared["weight"], at["own"], at["recv"], (1, 1), [(at["passed"], 1)], shared["after"]
        )
        at["last"] = hop(near, ends)
        shared["after"] = (kept,)

    def step_finish(c, at):
        shared["results"] = finish(
            shared["weight"],
            at["own"],
            at["recv"],
            at["passed"],
            at["last"],
            rows_all,
            starts[c] // sizes[c],
            shared["results"],
            shared["after"],
        )
        shared["after"] = shared["after"] + (at["last"],)

    def step_whole(c, at):
        result, kept = shrink(
            shared["weight"], at["own"], at["recv"], (0, line), (), shared["after"]
        )
        at["result"] = lax.psum_scatter(
            result, "blk", scatter_dimension=0, axis_index_groups=along
        )
        shared["after"] = (kept,)

    def step_outer(c, at):
        total, token = outer(
            flags, shared["weight"], at["own"], at["recv"], at["parts"], shared["total"], shared["after"]
        )
        shared["total"], shared["after"] = (total,), (token,)

    held = max(blocks // 2, 1)

    def step_inner(i, at):
        kept = [s["saved"] for s in state]
        first = i // held * held
        before = shared["inner"] if i > first else ()
        done = inner(kept, block_width, i, first, held, before, shared["after"])
        shared["inner"] = (done,)
        if i == first + held - 1:
            terms.append(done)

    def step_reduce(h, at):
        term, _ = lax.optimization_barrier((terms[h], shared["after"][0]))
        summed.append(lax.psum_scatter(term, "seq", scatter_dimension=1, tiled=True))

    steps = dict(
        G=step_gather, E=step_expand, M=step_middle, F=step_far, T=step_turn,
        N=step_near, D=step_finish, W=step_whole, O=step_outer, I=step_inner, R=step_reduce,
    )
    if short:
        plan = [("G", c) for c in range(count)]
        plan += [(w[0], int(w[1:])) for row in ORDER for half in row for w in half.split()]
    else:
        plan = [(k, c) for c in range(count) for k in "GEMWO"] + [("I", i) for i in range(blocks)]
        plan += [("R", h) for h in range(blocks // held)]
    for name, c in plan:
        steps[name](c, state[c] if c < count else None)
    total = shared["total"][0].astype(HALF)
    first = at_group % 2 == 0
    sent = jnp.where(first, total[1], total[0])
    kept = jnp.where(first, total[0], total[1]).astype(SINGLE)
    kept = kept + lax.ppermute(sent, "seq", [(k, k ^ 1) for k in range(groups)]).astype(SINGLE)
    kept = kept + lax.ppermute(kept.astype(HALF), "seq", [(2, 0), (1, 3)]).astype(SINGLE)
    kept = jnp.where(at_pair == 0, kept, jnp.roll(kept, width // 2, axis=2)).astype(HALF)
    kept = across(jnp.take(kept, jnp.argsort(order), axis=0))
    kept = jnp.take(kept, (at_line - jnp.arange(line)) % line, axis=0)
    kept = kept.transpose(1, 3, 0, 2).reshape(blocks, block_width, full)
    edges = jnp.stack([at_group == 0, at_group == groups - 1]).astype(jnp.int32)
    weight_grads = ()
    for first, part in enumerate(summed):
        weight_grads = (assemble(edges, part, kept, first * held, blocks, weight_grads),)
    weight_grads = weight_grads[0]
    if short:
        grad, result = shared["results"]
    else:
        result = jnp.concatenate([s["result"] for s in state], axis=1)
        grad, result = result[0], result[1]
    return result, grad, weight_grads


def solution(mesh):
    placed = (
        P("seq", "blk"),
        P("blk", None, None),
        P("blk", None, None),
        P("blk", None, None),
        P("blk", None, None),
        P("seq", "blk"),
    )
    return jax.shard_map(
        on_device,
        mesh=mesh,
        in_specs=placed,
        out_specs=(P("seq", "blk"), P("seq", "blk"), P("blk", "seq", None)),
        check_vma=False,
    )
```

```python
import functools

import jax
import jax.numpy as jnp
from jax import lax
from jax.experimental import pallas as pl
from jax.experimental.pallas import tpu as pltpu
from jax.sharding import PartitionSpec as P

PARTS = (1, 1, 1, 1)
ORDER = (
    ("E0 M0 E1", "F0 E2 M1", "T0 O0 M2", "N0 E3 F1"),
    ("O1 M3 D0", "F2 T1 I0", "I1 F3 N1", "T2 R0 O2"),
    ("O3 I2 N2", "I3 T3 R1", "D1 N3 D2 D3"),
)


PAIR = 2
VMEM = 62 * 1024 * 1024
SINGLE = jnp.float32
HALF = jnp.bfloat16


def dot(left, right, left_dim, right_dim):
    return lax.dot_general(
        left, right, (((left_dim,), (right_dim,)), ((), ())), preferred_element_type=SINGLE
    )


def params():
    return pltpu.CompilerParams(vmem_limit_bytes=VMEM)


def cost(*_):
    return pl.CostEstimate(flops=1024, bytes_accessed=1024, transcendentals=0)


def slot_of(order, parts, slot):
    return parts[0][order[slot], 0]


def part_specs(parts):
    line, _, rows, wide = parts[0].shape
    return [pl.BlockSpec((line, 1, rows, wide), lambda a, p: (0, a, 0, 0))]


def waits(after):
    return [pl.BlockSpec(memory_space=pl.ANY) for _ in after]


def expand_kernel(groups, count, flags, spots, *refs):
    shares, parts = refs[:groups], refs[groups : groups + count]
    own, send, weight = refs[-3:]
    line, blocks, width, block_width = weight.shape
    rows = own.shape[-2]
    piece = width // groups
    for n, share in enumerate(shares):
        place = pl.ds(pl.multiple_of(spots[n] * piece, piece), piece)
        for slot in range(line):
            for j in range(blocks):
                weight[slot, j, place, :] = share[spots[groups + slot], 0, j]
    for slot in range(line):
        here = slot_of(flags, parts, slot)
        for j in range(blocks):
            value = dot(
                weight[slot, j], here[:, j * block_width : (j + 1) * block_width], 1, 1
            ).astype(HALF)
            half = width // 2
            for i in range(blocks):
                own[0, i, slot, j] = value[i * rows : (i + 1) * rows]
                send[0, i, slot, j] = value[half + i * rows : half + (i + 1) * rows]


def expand(flags, spots, shares, parts, after):
    line, two, blocks, piece, block_width = shares[0].shape
    width = piece * len(shares)
    rows_here = parts[0].shape[-2]
    rows = width // (PAIR * blocks)
    shape = jax.ShapeDtypeStruct((two, blocks, line, blocks, rows, rows_here), HALF)
    out_spec = pl.BlockSpec((1,) + shape.shape[1:], lambda a, p, q: (a, 0, 0, 0, 0, 0))
    specs = [
        pl.BlockSpec(s.block_shape, lambda a, p, q, s=s: s.index_map(a, p)) for s in part_specs(parts)
    ]
    share_spec = pl.BlockSpec(
        (line, 1, blocks, piece, block_width), lambda a, p, q: (0, a, 0, 0, 0)
    )
    return pl.pallas_call(
        functools.partial(expand_kernel, len(shares), len(parts)),
        grid_spec=pltpu.PrefetchScalarGridSpec(
            num_scalar_prefetch=2,
            grid=(two,),
            in_specs=[share_spec] * len(shares) + specs + waits(after),
            out_specs=[out_spec, out_spec],
            scratch_shapes=[pltpu.VMEM((line, blocks, width, block_width), HALF)],
        ),
        out_shape=[shape, shape],
        compiler_params=params(),
        cost_estimate=cost(1),
        name="expand",
    )(flags, spots, *shares, *parts, *after)


def middle_kernel(places, own, recv, up, down, *refs):
    own_out, send_out, saved, result = refs[-4:]
    line, rows = own.shape[2], own.shape[3]

    def spot(half, slot):
        return pl.ds(pl.multiple_of(places[half * line + slot] * rows, rows), rows)

    for half, source in enumerate((own, recv)):
        for slot in range(line):
            saved[0, 0, 0, spot(half, slot), :] = source[0, 0, slot]
            saved[1, 1, 0, spot(half, slot), :] = source[1, 0, slot]
    before = dot(up[0], saved[0, 0, 0], 0, 0)
    bell = 0.5 * (1.0 + lax.erf(before * 0.7071067811865476))
    slope = bell + before * jnp.exp(-0.5 * before * before) * 0.3989422804014327
    saved[1, 0, 0] = (before * bell).astype(HALF)
    grad_act = dot(down[0], saved[1, 1, 0], 1, 0)
    saved[0, 1, 0] = (grad_act * slope).astype(HALF)
    result[0] = dot(up[0], saved[0, 1, 0], 1, 0).astype(HALF)
    result[1] = dot(down[0], saved[1, 0, 0], 0, 0).astype(HALF)
    for half, target in enumerate((own_out, send_out)):
        for slot in range(line):
            for a in range(2):
                target[a, 0, slot] = result[a, spot(half, slot), :]


def middle(places, own, recv, up, down, after):
    two, blocks, line, rows, rows_here = own.shape
    full = up.shape[1]
    part = pl.BlockSpec((two, 1, line, rows, rows_here), lambda i, p: (0, i, 0, 0, 0))
    factor = pl.BlockSpec((1, full, full), lambda i, p: (i, 0, 0))
    shape = jax.ShapeDtypeStruct(own.shape, HALF)
    kept = jax.ShapeDtypeStruct((2, 2, blocks, full, rows_here), HALF)
    return pl.pallas_call(
        middle_kernel,
        grid_spec=pltpu.PrefetchScalarGridSpec(
            num_scalar_prefetch=1,
            grid=(blocks,),
            in_specs=[part, part, factor, factor] + waits(after),
            out_specs=[
                part,
                part,
                pl.BlockSpec((2, 2, 1, full, rows_here), lambda i, p: (0, 0, i, 0, 0)),
            ],
            scratch_shapes=[pltpu.VMEM((2, full, rows_here), HALF)],
        ),
        out_shape=[shape, shape, kept],
        compiler_params=params(),
        cost_estimate=cost(8 * up.size * rows_here, own, recv, up, up, down, down, shape, shape, kept),
        name="middle",
    )(places, own, recv, up, down, *after)


def hidden(own, recv, a, slot, j):
    blocks, rows, rows_here = own.shape[1], own.shape[4], own.shape[5]
    return jnp.concatenate(
        [r[a, :, slot, j].reshape(blocks * rows, rows_here) for r in (own, recv)], axis=0
    )


def shrink_kernel(count, weight, own, recv, *rest):
    added, out, keep = rest[:count], rest[-2], rest[-1]
    blocks, block_width = weight.shape[2], weight.shape[-1]
    for j in range(blocks):
        at = slice(j * block_width, (j + 1) * block_width)
        value = dot(hidden(own, recv, 0, 0, j), weight[0, 0, j], 0, 0)
        for ref in added:
            value = value + ref[0, 0, :, at].astype(SINGLE)
        out[0, 0, :, at] = value.astype(HALF)
        if keep.shape == out.shape:
            keep[0, 0, :, at] = value.astype(HALF)
    if keep.shape != out.shape:
        keep[...] = jnp.zeros_like(keep)


def shrink(weight, own, recv, slots, added=(), after=(), twice=False):
    two, line, blocks, width, block_width = weight.shape
    rows, rows_here = own.shape[4:]
    first, count = slots
    shape = jax.ShapeDtypeStruct((count, two, rows_here, blocks * block_width), HALF)
    part = pl.BlockSpec(
        (1, blocks, 1, blocks, rows, rows_here), lambda s, a: (a, 0, s + first, 0, 0, 0)
    )

    def block(at):
        return pl.BlockSpec(
            (1, 1, rows_here, blocks * block_width), lambda s, a: (s + at, a, 0, 0)
        )

    return pl.pallas_call(
        functools.partial(shrink_kernel, len(added)),
        grid=(count, two),
        in_specs=[
            pl.BlockSpec((1, 1, blocks, width, block_width), lambda s, a: (a, s + first, 0, 0, 0)),
            part,
            part,
        ]
        + [block(at) for _, at in added]
        + waits(after),
        out_specs=[block(0), block(0) if twice else pl.BlockSpec((8, 128), lambda s, a: (0, 0))],
        out_shape=[shape, shape if twice else jax.ShapeDtypeStruct((8, 128), SINGLE)],
        compiler_params=params(),
        cost_estimate=cost(
            2 * count * weight.size // line * rows_here, shape, shape, *[shape for _ in added]
        ),
        name="shrink",
    )(weight, own, recv, *[a for a, _ in added], *after)


def join_kernel(left, right, *rest):
    out, token = rest[-2:]
    out[...] = left[...] + right[...]
    token[...] = jnp.zeros_like(token)


def join(left, right, after):
    spec = pl.BlockSpec((1,) + left.shape[1:], lambda s: (s, 0, 0, 0))
    return pl.pallas_call(
        join_kernel,
        grid=left.shape[:1],
        in_specs=[spec, spec] + waits(after),
        out_specs=[spec, pl.BlockSpec((8, 128), lambda s: (0, 0))],
        out_shape=[
            jax.ShapeDtypeStruct(left.shape, HALF),
            jax.ShapeDtypeStruct((8, 128), SINGLE),
        ],
        compiler_params=params(),
        cost_estimate=cost(1),
        name="join",
    )(left, right, *after)


def finish_kernel(weight, own, recv, passed, last, *rest):
    blocks, block_width = weight.shape[2], weight.shape[-1]
    for a, out in enumerate(rest[-2:]):
        for j in range(blocks):
            at = slice(j * block_width, (j + 1) * block_width)
            value = dot(hidden(own, recv, a, 0, j), weight[a, 0, j], 0, 0)
            value = value + passed[0, a, :, at].astype(SINGLE) + last[0, a, :, at].astype(SINGLE)
            out[:, at] = value.astype(HALF)


def finish(weight, own, recv, passed, last, rows_all, at, before, after):
    two, line, blocks, width, block_width = weight.shape
    rows, rows_here = own.shape[4:]
    wide = blocks * block_width
    shape = jax.ShapeDtypeStruct((rows_all, wide), HALF)
    part = pl.BlockSpec((two, blocks, 1, blocks, rows, rows_here), lambda s: (0, 0, 0, 0, 0, 0))
    block = pl.BlockSpec((1, two, rows_here, wide), lambda s: (0, 0, 0, 0))
    out_spec = pl.BlockSpec((rows_here, wide), lambda s: (at, 0))
    return pl.pallas_call(
        finish_kernel,
        grid=(1,),
        in_specs=[
            pl.BlockSpec((two, 1, blocks, width, block_width), lambda s: (0, 0, 0, 0, 0)),
            part,
            part,
            block,
            block,
        ]
        + waits(before)
        + waits(after),
        out_specs=[out_spec, out_spec],
        out_shape=[shape, shape],
        input_output_aliases={5: 0, 6: 1} if before else {},
        compiler_params=params(),
        cost_estimate=cost(2 * weight.size // line * rows_here, passed, last),
        name="finish",
    )(weight, own, recv, passed, last, *before, *after)


def outer_kernel(count, more, flags, own, recv, *refs):
    parts, before = refs[:count], refs[count : count + more]
    out, token = refs[-2:]
    line, blocks, _, block_width = out.shape[1:]
    token[...] = jnp.zeros_like(token)
    for slot in range(line):
        here = slot_of(flags, parts, slot)
        for j in range(blocks):
            value = dot(
                hidden(own, recv, 0, slot, j),
                here[:, j * block_width : (j + 1) * block_width],
                1,
                0,
            )
            for ref in before:
                value = value + ref[0, slot, j]
            out[0, slot, j] = value


def outer(flags, weight, own, recv, parts, before, after):
    rows_here = own.shape[5]
    part = pl.BlockSpec((1,) + own.shape[1:], lambda a, p: (a, 0, 0, 0, 0, 0))
    shape = jax.ShapeDtypeStruct(weight.shape, SINGLE)
    total = pl.BlockSpec((1,) + weight.shape[1:], lambda a, p: (a, 0, 0, 0, 0))
    return pl.pallas_call(
        functools.partial(outer_kernel, len(parts), len(before)),
        grid_spec=pltpu.PrefetchScalarGridSpec(
            num_scalar_prefetch=1,
            grid=(weight.shape[0],),
            in_specs=[part, part]
            + part_specs(parts)
            + [total for _ in before]
            + waits(after),
            out_specs=[total, pl.BlockSpec((8, 128), lambda a, p: (0, 0))],
        ),
        out_shape=[shape, jax.ShapeDtypeStruct((8, 128), SINGLE)],
        input_output_aliases={3 + len(parts): 0} if before else {},
        compiler_params=params(),
        cost_estimate=cost(2 * weight.size * rows_here, own, recv, *parts, shape, shape),
        name="outer",
    )(flags, own, recv, *parts, *before, *after)


def inner_kernel(count, *refs):
    saved, out = refs[: 2 * count], refs[-1]
    m = pl.program_id(0)
    last = pl.num_programs(0) - 1
    edge = (m == 0) | (m == last)

    @pl.when(edge)
    def _():
        out[...] = jnp.zeros_like(out)

    @pl.when(jnp.logical_not(edge))
    def _():
        value, held = 0.0, []
        for left, right in zip(saved[::2], saved[1::2]):
            held.append((left[0, 0, 0], right[0, 0, 0]))
            if sum(h[0].shape[1] for h in held) >= 256:
                left, right = (jnp.concatenate(v, axis=1) for v in zip(*held))
                value, held = value + dot(left, right, 1, 1), []
        out[0] = value.astype(HALF)


def inner(saved, block_width, i, first, held, before, after):
    _, _, blocks, full, _ = saved[0].shape
    per = full // block_width
    steps = 2 * per + 2

    def at(m):
        row = jnp.clip(m - 1, 0, 2 * per - 1)
        return row // per, row % per

    specs = []
    for s in saved:
        left = (1, 1, 1, block_width, s.shape[-1])
        right = (1, 1, 1, full, s.shape[-1])
        specs.append(pl.BlockSpec(left, lambda m: (at(m)[0], 0, i, at(m)[1], 0)))
        specs.append(pl.BlockSpec(right, lambda m: (at(m)[0], 1, i, 0, 0)))
    return pl.pallas_call(
        functools.partial(inner_kernel, len(saved)),
        grid=(steps,),
        in_specs=specs + waits(before) + waits(after),
        out_specs=pl.BlockSpec((1, block_width, full), lambda m: (i - first, m, 0)),
        out_shape=jax.ShapeDtypeStruct((held, steps * block_width, full), HALF),
        input_output_aliases={2 * len(saved): 0} if before else {},
        compiler_params=params(),
        cost_estimate=cost(1),
        name="inner",
    )(*[s for s in saved for _ in range(2)], *before, *after)


def assemble_kernel(edges, summed, kept, *rest):
    out = rest[-1]
    width = kept.shape[1]
    out[...] = summed[...].astype(SINGLE)

    @pl.when(edges[0] == 1)
    def _():
        out[:, :width] = kept[...].astype(SINGLE)

    @pl.when(edges[1] == 1)
    def _():
        out[:, out.shape[1] - width :] = kept[...].astype(SINGLE)


def assemble(edges, summed, kept, first, blocks, before):
    held, rows, full = summed.shape
    wide = 256
    spec = pl.BlockSpec((1, rows, wide), lambda i, c, p: (i, 0, c))
    return pl.pallas_call(
        assemble_kernel,
        grid_spec=pltpu.PrefetchScalarGridSpec(
            num_scalar_prefetch=1,
            grid=(held, full // wide),
            in_specs=[
                spec,
                pl.BlockSpec((1, kept.shape[1], wide), lambda i, c, p: (i + first, 0, c)),
            ]
            + waits(before),
            out_specs=pl.BlockSpec((1, rows, wide), lambda i, c, p: (i + first, 0, c)),
        ),
        out_shape=jax.ShapeDtypeStruct((blocks, rows, full), SINGLE),
        input_output_aliases={3: 0} if before else {},
        compiler_params=params(),
        cost_estimate=cost(1),
        name="assemble",
    )(edges, summed, kept, *before)


def on_device(tokens, up_in, up_out, down_in, down_out, cotangent):
    rows_all = tokens.shape[0]
    blocks, block_width, full = up_in.shape
    peers, groups = lax.axis_size("blk"), lax.axis_size("seq")
    line = peers // PAIR
    piece = full // (blocks * peers)
    width = PAIR * blocks * piece
    rows = blocks * piece
    at_line, at_pair = lax.axis_index("blk") // PAIR, lax.axis_index("blk") % PAIR
    at_group = lax.axis_index("seq")
    along = [[o * PAIR + q for o in range(line)] for q in range(PAIR)]
    parts = PARTS
    sizes = [rows_all * k // sum(parts) for k in parts]
    starts = [sum(sizes[:c]) for c in range(len(sizes))]
    count = len(sizes)
    short = line == 4

    def lines(pairs):
        return [(a * PAIR + q, b * PAIR + q) for a, b in pairs for q in range(PAIR)]

    def hop(value, pairs):
        return lax.ppermute(value, "blk", lines(pairs))

    def other(value):
        return lax.ppermute(value, "blk", [(k, k ^ 1) for k in range(peers)])

    ends, turn = [(0, 1), (1, 0), (2, 3), (3, 2)], [(1, 2), (2, 1)]
    inward = [(0, 1), (3, 2)]
    if short:
        order = jnp.array([[0, 1, 2, 3], [1, 0, 2, 3], [2, 3, 1, 0], [3, 2, 1, 0]], jnp.int32)[
            at_line
        ]
    else:
        order = jnp.arange(line, dtype=jnp.int32)
    flags = order
    places = jnp.concatenate([order * PAIR + at_pair, order * PAIR + 1 - at_pair])

    def across(pieces):
        if not short:
            moved = lax.all_to_all(pieces, "blk", 0, 0, axis_index_groups=along, tiled=True)
            return jnp.take(moved, (at_line - jnp.arange(line)) % line, axis=0)
        moved = []
        for far in range(line):
            piece_at = lax.dynamic_index_in_dim(pieces, (at_line + far) % line, 0, keepdims=False)
            moved.append(hop(piece_at, [(k, (k + far) % line) for k in range(line)]) if far else piece_at)
        return jnp.stack(moved)

    chunks = [jnp.stack([v[k : k + n] for v in (tokens, cotangent)]) for k, n in zip(starts, sizes)]

    def step_gather(c, at):
        mine = chunks[c]
        if shared["total"] and not short:
            mine, _ = lax.optimization_barrier((mine, shared["total"][0]))
        at["parts"] = [lax.all_gather(mine, "blk", axis_index_groups=along)]

    factors = jnp.stack([up_in, down_out]).reshape(
        2, blocks, block_width, line, groups, width // groups
    )
    share = lax.dynamic_index_in_dim(factors, at_group, 4, keepdims=False)
    share = across(share.transpose(3, 0, 1, 4, 2))
    shares = [share, lax.ppermute(share, "seq", [(k, k ^ 2) for k in range(groups)])]
    shares += [lax.ppermute(v, "seq", [(k, k ^ 1) for k in range(groups)]) for v in shares]
    whose = at_group ^ jnp.array([0, 2, 1, 3], jnp.int32)
    stand = (whose + at_pair * (groups // 2)) % groups
    source = (at_line - order) % line
    spots = jnp.concatenate([stand, source]).astype(jnp.int32)
    def whole_weight(first):
        held, _ = lax.optimization_barrier((tuple(shares), first))
        held = jnp.stack(held)[jnp.argsort(stand)][:, source]
        held = held.transpose(2, 1, 3, 0, 4, 5)
        return held.reshape(2, line, blocks, width, block_width)

    flat = (2, blocks, line, rows, -1)
    deep = (2, blocks, line, blocks, piece, -1)
    state = [dict() for _ in range(count)]
    terms, summed = [], []
    shared = {"after": (), "results": (), "total": (), "inner": ()}

    def step_expand(c, at):
        at["own"], send = expand(flags, spots, shares, at["parts"], shared["after"])
        at["recv"] = other(send)
        shared["after"] = (at["own"],)
        if c == 0:
            shared["weight"] = whole_weight(at["own"])

    def step_middle(c, at):
        own, send, at["saved"] = middle(
            places,
            at["own"].reshape(flat),
            at["recv"].reshape(flat),
            up_out,
            down_in,
            shared["after"] + ((shared["weight"],) if c == 0 else ()),
        )
        at["own"], at["recv"] = own.reshape(deep), other(send).reshape(deep)
        shared["after"] = (own,)

    def step_far(c, at):
        sent, at["sum"] = shrink(
            shared["weight"], at["own"], at["recv"], (2, 2), (), shared["after"], twice=True
        )
        at["arrived"] = hop(sent, inward)
        shared["after"] = (at["sum"],)

    def step_turn(c, at):
        both, token = join(at["sum"], at["arrived"], shared["after"])
        at["passed"] = hop(both, turn)
        shared["after"] = (token,)

    def step_near(c, at):
        near, kept = shrink(
            shared["weight"], at["own"], at["recv"], (1, 1), [(at["passed"], 1)], shared["after"]
        )
        at["last"] = hop(near, ends)
        shared["after"] = (kept,)

    def step_finish(c, at):
        shared["results"] = finish(
            shared["weight"],
            at["own"],
            at["recv"],
            at["passed"],
            at["last"],
            rows_all,
            starts[c] // sizes[c],
            shared["results"],
            shared["after"],
        )
        shared["after"] = shared["after"] + (at["last"],)

    def step_whole(c, at):
        result, kept = shrink(
            shared["weight"], at["own"], at["recv"], (0, line), (), shared["after"]
        )
        at["result"] = lax.psum_scatter(
            result, "blk", scatter_dimension=0, axis_index_groups=along
        )
        shared["after"] = (kept,)

    def step_outer(c, at):
        total, token = outer(
            flags, shared["weight"], at["own"], at["recv"], at["parts"], shared["total"], shared["after"]
        )
        shared["total"], shared["after"] = (total,), (token,)

    held = max(blocks // 2, 1)

    def step_inner(i, at):
        kept = [s["saved"] for s in state]
        first = i // held * held
        before = shared["inner"] if i > first else ()
        done = inner(kept, block_width, i, first, held, before, shared["after"])
        shared["inner"] = (done,)
        if i == first + held - 1:
            terms.append(done)

    def step_reduce(h, at):
        term, _ = lax.optimization_barrier((terms[h], shared["after"][0]))
        summed.append(lax.psum_scatter(term, "seq", scatter_dimension=1, tiled=True))

    steps = dict(
        G=step_gather, E=step_expand, M=step_middle, F=step_far, T=step_turn,
        N=step_near, D=step_finish, W=step_whole, O=step_outer, I=step_inner, R=step_reduce,
    )
    if short:
        plan = [("G", c) for c in range(count)]
        plan += [(w[0], int(w[1:])) for row in ORDER for half in row for w in half.split()]
    else:
        plan = [(k, c) for c in range(count) for k in "GEMWO"] + [("I", i) for i in range(blocks)]
        plan += [("R", h) for h in range(blocks // held)]
    for name, c in plan:
        steps[name](c, state[c] if c < count else None)
    total = shared["total"][0].astype(HALF)
    first = at_group % 2 == 0
    sent = jnp.where(first, total[1], total[0])
    kept = jnp.where(first, total[0], total[1]).astype(SINGLE)
    kept = kept + lax.ppermute(sent, "seq", [(k, k ^ 1) for k in range(groups)]).astype(SINGLE)
    kept = kept + lax.ppermute(kept.astype(HALF), "seq", [(2, 0), (1, 3)]).astype(SINGLE)
    kept = jnp.where(at_pair == 0, kept, jnp.roll(kept, width // 2, axis=2)).astype(HALF)
    kept = across(jnp.take(kept, jnp.argsort(order), axis=0))
    kept = jnp.take(kept, (at_line - jnp.arange(line)) % line, axis=0)
    kept = kept.transpose(1, 3, 0, 2).reshape(blocks, block_width, full)
    edges = jnp.stack([at_group == 0, at_group == groups - 1]).astype(jnp.int32)
    weight_grads = ()
    for first, part in enumerate(summed):
        weight_grads = (assemble(edges, part, kept, first * held, blocks, weight_grads),)
    weight_grads = weight_grads[0]
    if short:
        grad, result = shared["results"]
    else:
        result = jnp.concatenate([s["result"] for s in state], axis=1)
        grad, result = result[0], result[1]
    return result, grad, weight_grads


def solution(mesh):
    placed = (
        P("seq", "blk"),
        P("blk", None, None),
        P("blk", None, None),
        P("blk", None, None),
        P("blk", None, None),
        P("seq", "blk"),
    )
    return jax.shard_map(
        on_device,
        mesh=mesh,
        in_specs=placed,
        out_specs=(P("seq", "blk"), P("seq", "blk"), P("blk", "seq", None)),
        check_vma=False,
    )
```
